256 devices in a mesh: replica: 16 (over z_hi, x, core), fsdp: 16 (over y, z_lo).
Axes of the slice: x: 4, y: 4, z: 8 (z_hi: 2, z_lo: 4; z = z_hi * 4 + z_lo), core: 2. Of those that a mesh axis runs over, the one named last changes fastest.
Arguments:
- pre_act: bfloat16 [16, 2048, 14336], P('replica', 'fsdp'), may hold values from -6 to 6
- out_grad: bfloat16 [16, 2048, 4096], P('replica', 'fsdp'), may hold values from -0.3125 to 0.3125
- pseudo_grads: float32 [16, 16, 65536], P('replica', 'fsdp'), may hold values from -6 to 6
- outer_params: float32 [16, 65536], P('fsdp'), may hold values from -4 to 4
- momentum: float32 [16, 65536], P('fsdp', 'replica'), may hold values from -6 to 6
Outputs:
- weight_grad: bfloat16 [16, 14336, 4096], P('replica', 'fsdp')
- new_moment: float32 [16, 65536], P('fsdp', 'replica')
- new_params: float32 [16, 65536], P('fsdp')
The draws below stay inside these ranges and needn't reach their ends.
All inputs are finite; a program needn't handle non-finite values.
Results may differ from the reference program's by a relative error of at most 0.01.
Values may be sent and summed in bfloat16 or wider, within the bound.
No kernel may reach another device: no remote copies, remote signals or barrier semaphores. Data moves between devices by JAX's collectives and lax.ppermute only.
A program may use at most 128 MiB of HBM per device.

```python
import jax
import jax.numpy as jnp
from jax import lax

D = 4096
FF = 14336
TOK_DEV = 128
FRAG_DEV = 65536
REPLICAS = 16
BLOCKS = 16
TOKENS = 2048
N_REPLICA = 16
N_FSDP = 16


def raised(entries, rng, source, target, parts, factor):
    owner, partner = [(jnp.arange(entries.shape[dim]) // (entries.shape[dim] // parts)).reshape([-1 if axis == dim else 1 for axis in range(entries.ndim)]) for dim in (source, target)]
    chosen = jax.random.permutation(rng, parts)[partner]
    strong = (owner == chosen) | (owner == (partner + parts // 2) % parts)
    return jnp.where(strong, factor * entries, entries)


def shard_levels(stream_key, extent, split, low, high):
    level, own = 1.0, jax.random.fold_in(stream_key, 6)
    for position, parts in split:
        draws = jnp.exp(jax.random.uniform(jax.random.fold_in(own, position), (parts,), jnp.float32, low / len(split), high / len(split)))
        level = level * jnp.repeat(draws, extent[position] // parts).reshape([-1 if axis == position else 1 for axis in range(len(extent))])
    return level


def normal_values(own_key, extent, scale, reach, split=(), dtype=jnp.bfloat16):
    values = jax.random.normal(own_key, extent, jnp.float32) * scale
    if len(split) > 0:
        values = shard_levels(own_key, extent, split, -0.22, 0.18) * values
    return jnp.clip(values, min=-reach, max=reach).astype(dtype)


def bell_draw_with(key, shape, scale, most, shards, heavy, dtype=jnp.bfloat16):
    result = scale * jax.random.normal(key, shape, jnp.float32)
    if shards:
        result = result * shard_levels(key, shape, shards, -0.22, 0.18)
    return jnp.clip(raised(result, jax.random.fold_in(key, 3), *heavy), -most, most).astype(dtype)


def setup_inputs(seed: int = 0) -> dict:
    key_of = jax.random.split(jax.random.key(seed), 6)
    pre_act = normal_values(key_of[0], (REPLICAS, TOKENS, FF), 1.0, 6.0, ((0, 16), (1, 16)))
    out_grad = normal_values(key_of[1], (REPLICAS, TOKENS, D), ((TOK_DEV * N_FSDP) ** -0.5), 0.3125, ((0, 16), (1, 16)))
    pseudo_grads = bell_draw_with(key_of[2], (REPLICAS, BLOCKS, FRAG_DEV), 1.0, 6.0, ((0, 16), (1, 16)), (0, 2, 16, 2.0), jnp.float32)
    outer_params = normal_values(key_of[3], (BLOCKS, FRAG_DEV), 0.5, 4.0, ((0, 16),), jnp.float32)
    momentum = normal_values(key_of[4], (BLOCKS, FRAG_DEV), 1.0, 6.0, ((0, 16), (1, 16)), jnp.float32)
    return dict(pre_act=pre_act, out_grad=out_grad, pseudo_grads=pseudo_grads, outer_params=outer_params, momentum=momentum)


outer_mu = 0.9
outer_lr = 0.7


def replica_step(operands):
    hidden, incoming = operands
    activated = jax.nn.silu(hidden.astype(jnp.float32)).astype(jnp.bfloat16)
    summed = lax.dot_general(activated, incoming, (((0,), (0,)), ((), ())), preferred_element_type=jnp.float32)
    return summed.astype(jnp.bfloat16)


def reference(pre_act, out_grad, pseudo_grads, outer_params, momentum):
    weight_grad = lax.map(replica_step, (pre_act, out_grad))
    delta = jnp.sum(pseudo_grads, axis=0) / N_REPLICA
    new_moment = outer_mu * momentum + delta
    new_params = outer_params - outer_lr * (delta + outer_mu * new_moment)
    return weight_grad, new_moment, new_params
```

```python
import jax
import jax.numpy as jnp
from jax import lax
from jax.experimental import pallas as pl
from jax.experimental.pallas import tpu as pltpu
from jax.sharding import PartitionSpec as P

outer_mu = 0.9
outer_lr = 0.7

NY, NZ = 4, 4
HALF = 2048
UNITS = 896
TOK = 128
LANES = 128
VMEM = 40 * 1024 * 1024
ORDER = [(k, d) for k in range(NZ) for d in (0, 1, 3, 2)]


def shift(dy, dz):
    return [
        (y * NZ + z, (y + dy) % NY * NZ + (z + dz) % NZ)
        for y in range(NY)
        for z in range(NZ)
    ]


def fsdp_send(array, dy, dz):
    return lax.ppermute(array, "fsdp", shift(dy, dz))


def replica_swap(array, bit):
    return lax.ppermute(array, "replica", [(r, r ^ bit) for r in range(16)])


def activate_kernel(place_ref, *refs):
    for source, target in zip(refs[:NY], refs[NY:]):
        value = source[0].astype(jnp.float32)
        value = value / (1.0 + jnp.exp(-value))
        target[0] = value.T.astype(jnp.bfloat16)


def activate(pre_act, place):
    def column(d):
        return lambda j, p: (0, 0, (p[0] + d) % NY * NZ + (p[1] + j) % NZ)

    return pl.pallas_call(
        activate_kernel,
        grid_spec=pltpu.PrefetchScalarGridSpec(
            num_scalar_prefetch=1,
            grid=(NZ,),
            in_specs=[pl.BlockSpec((1, TOK, UNITS), column(d)) for d in range(NY)],
            out_specs=[
                pl.BlockSpec((1, UNITS, TOK), lambda j, p: (j, 0, 0))
                for _ in range(NY)
            ],
        ),
        out_shape=[jax.ShapeDtypeStruct((NZ, UNITS, TOK), jnp.bfloat16)] * NY,
        compiler_params=pltpu.CompilerParams(vmem_limit_bytes=VMEM),
    )(place, *[pre_act] * NY)


def most_kernel(count, lefts, *refs):
    sources, rights = refs[: len(lefts)], refs[len(lefts) : -2]
    out_ref, packed = refs[-2:]

    @pl.when(pl.program_id(0) == 0)
    def _():
        for i, (source, (_, row)) in enumerate(zip(sources, lefts)):
            packed[:, i * TOK : (i + 1) * TOK] = source[0]

    right = jnp.concatenate([r[0] for r in rights], axis=0)
    out_ref[...] = jnp.dot(packed[...], right, preferred_element_type=jnp.float32)


def most(lefts, rights, width):
    count = len(lefts)
    return pl.pallas_call(
        lambda *refs: most_kernel(count, lefts, *refs),
        grid=(HALF // width,),
        in_specs=[
            pl.BlockSpec((1, UNITS, TOK), lambda n, row=row: (row, 0, 0))
            for _, row in lefts
        ]
        + [pl.BlockSpec((1, r.shape[1], width), lambda n: (0, 0, n)) for r in rights],
        out_specs=pl.BlockSpec((UNITS, width), lambda n: (0, n)),
        out_shape=jax.ShapeDtypeStruct((UNITS, HALF), jnp.float32),
        scratch_shapes=[pltpu.VMEM((UNITS, count * TOK), jnp.bfloat16)],
        compiler_params=pltpu.CompilerParams(vmem_limit_bytes=VMEM),
        cost_estimate=pl.CostEstimate(
            flops=2 * UNITS * HALF * count * TOK,
            bytes_accessed=UNITS * HALF * 4 + count * TOK * (HALF + UNITS) * 2,
            transcendentals=0,
        ),
    )(*[a for a, _ in lefts], *rights)


def last_kernel(left, top, bottom, total, *rest):
    out_ref = rest[-1]
    right = jnp.concatenate([top[0], bottom[0]], axis=0)
    value = total[...] + jnp.dot(left[0], right, preferred_element_type=jnp.float32)
    out_ref[0] = value.astype(jnp.bfloat16)


def last(left, top, bottom, total, half, out, width):
    array, row = left
    first = half * (HALF // width)
    operands = [array, top, bottom, total]
    in_specs = [
        pl.BlockSpec((1, UNITS, TOK), lambda n: (row, 0, 0)),
        pl.BlockSpec((1, TOK // 2, width), lambda n: (0, 0, n)),
        pl.BlockSpec((1, TOK // 2, width), lambda n: (0, 0, n)),
        pl.BlockSpec((UNITS, width), lambda n: (0, n)),
    ]
    alias = {}
    if out is not None:
        operands.append(out)
        in_specs.append(pl.BlockSpec(memory_space=pl.ANY))
        alias = {4: 0}
    return pl.pallas_call(
        last_kernel,
        grid=(HALF // width,),
        in_specs=in_specs,
        out_specs=pl.BlockSpec((1, UNITS, width), lambda n: (0, 0, first + n)),
        out_shape=jax.ShapeDtypeStruct((1, UNITS, 2 * HALF), jnp.bfloat16),
        input_output_aliases=alias,
        compiler_params=pltpu.CompilerParams(vmem_limit_bytes=VMEM),
        cost_estimate=pl.CostEstimate(
            flops=2 * UNITS * HALF * TOK,
            bytes_accessed=UNITS * HALF * 6,
            transcendentals=0,
        ),
    )(*operands)


class Outer:
    def __init__(self, pseudo_grads, outer_params, momentum):
        self.bits = []
        index = lax.axis_index("replica")
        for bit in (1, 2, 4, 8):
            self.bits.append((index // bit) % 2)
        self.index = index
        self.held = pseudo_grads.reshape(2, 2, 2, 2, 32, LANES)
        self.outer_params, self.momentum = outer_params, momentum
        self.stage = 0
        self.pending = None

    def outgoing(self):
        if self.stage < 4:
            axis = 3 - self.stage
            mine = self.bits[self.stage]
            self.keep = lax.dynamic_index_in_dim(self.held, mine, axis, False)
            return lax.dynamic_index_in_dim(self.held, 1 - mine, axis, False)
        return self.held

    def exchange(self, sent):
        bit = (1, 2, 4, 8, 8, 4, 2, 1)[self.stage]
        return replica_swap(sent, bit)

    def incoming(self, received):
        if self.stage < 4:
            self.held = self.keep + received
            if self.stage == 3:
                self.update()
        else:
            mine = self.bits[7 - self.stage]
            axis = self.stage - 4
            low = jnp.where(mine == 0, self.held, received)
            high = jnp.where(mine == 0, received, self.held)
            self.held = jnp.stack([low, high], axis=axis)
        self.stage += 1

    def update(self):
        replicas = lax.axis_size("replica")
        share = self.momentum.shape[1]
        delta = self.held / replicas
        old_moment = self.momentum.reshape(32, LANES)
        moment = outer_mu * old_moment + delta
        old = lax.dynamic_slice_in_dim(
            self.outer_params[0], self.index * share, share, 0
        ).reshape(32, LANES)
        self.moment = moment
        self.held = old - outer_lr * (delta + outer_mu * moment)

    def results(self):
        return self.moment.reshape(1, -1), self.held.reshape(1, -1)


def on_device(pre_act, out_grad, pseudo_grads, outer_params, momentum):
    fsdp = lax.axis_index("fsdp")
    place = jnp.stack([fsdp // NZ, fsdp % NZ]).astype(jnp.int32)
    outer = Outer(pseudo_grads, outer_params, momentum)
    env = {}
    halves = "AB"
    for h, name in enumerate(halves):
        env["b0" + name] = out_grad[:, :, h * HALF : (h + 1) * HALF]

    def relay(name, side):
        return env[name][:, : TOK // 2] if side > 0 else env[name][:, TOK // 2 :]

    groups = []

    def transfer(*items):
        sources = [item[1]() for item in items]
        swap = None
        if outer.stage < 8:
            swap = outer.outgoing()
            sources.append(swap)
        earlier = groups[-2] if len(groups) >= 2 else []
        held = lax.optimization_barrier(
            tuple(sources) + tuple(env[name] for name in earlier)
        )
        for name, value in zip(earlier, held[len(sources) :]):
            env[name] = value
        made = []
        for (name, _, dy, dz), source in zip(items, held):
            env[name] = fsdp_send(source, dy, dz)
            made.append(name)
        if swap is not None:
            outer.incoming(outer.exchange(held[len(items)]))
        groups.append(made)

    def up(k, name):
        return [
            (f"p{k}{name}", lambda: env[f"b{k}{name}"], 1, 0),
            (f"m{k}{name}", lambda: env[f"b{k}{name}"], -1, 0),
        ]

    def on(k, name):
        return [
            (f"P{k}{name}", lambda: relay(f"p{k}{name}", 1), 1, 0),
            (f"M{k}{name}", lambda: relay(f"m{k}{name}", -1), -1, 0),
        ]

    def along(k, name):
        return [(f"b{k}{name}", lambda: env[f"b{k - 1}{name}"], 0, 1)]

    def spread(s, parts, name):
        def packed():
            return jnp.stack([env[f"R{d}"][s] for d in parts])

        return [(name, packed, 0, s)]

    env["R0"], env["o1"], env["o2"], env["o3"] = activate(pre_act, place)
    acts = [
        ("R1", lambda: env["o1"], 1, 0),
        ("R3", lambda: env["o3"], -1, 0),
    ]
    acts_far = [
        ("q2", lambda: env["o2"][:2], 1, 0),
        ("w2", lambda: env["o2"][2:], -1, 0),
    ]
    acts_on = [
        ("Q2", lambda: env["q2"], 1, 0),
        ("W2", lambda: env["w2"], -1, 0),
    ]

    transfer(*along(1, "A"), *up(0, "A"))
    transfer(*along(1, "B"), *acts_far, *up(0, "B"))
    transfer(*along(2, "A"), *acts)
    transfer(*along(2, "B"), *acts_on, *on(0, "A"))
    transfer(*along(3, "A"), *on(0, "B"), *up(1, "A"))
    env["R2"] = jnp.concatenate([env["Q2"], env["W2"]])
    every = range(NY)
    transfer(*along(3, "B"), *on(1, "A"), *up(1, "B"))
    transfer(*spread(1, every, "X1"), *on(1, "B"), *up(2, "A"))
    transfer(*spread(2, (0, 1), "X2a"), *spread(3, (0, 1), "X3a"), *on(2, "A"), *up(2, "B"))
    transfer(*spread(2, (2, 3), "X2b"), *spread(3, (2, 3), "X3b"), *on(2, "B"), *up(3, "A"))
    transfer(*on(3, "A"), *up(3, "B"))
    transfer(*on(3, "B"))

    def left(k, d):
        if k == 0:
            return env[f"R{d}"], 0
        if k == 1:
            return env["X1"], d
        return env[f"X{k}" + "ab"[d // 2]], d % 2

    def right(k, d, name):
        if d == 0:
            return [env[f"b{k}{name}"]]
        if d == 2:
            return [env[f"P{k}{name}"], env[f"M{k}{name}"]]
        return [env[("p" if d == 1 else "m") + f"{k}{name}"]]

    weight_grad = None
    for h, name in enumerate(halves):
        lefts = [left(*block) for block in ORDER[:-1]]
        rights = [r for block in ORDER[:-1] for r in right(*block, name)]
        total = most(lefts, rights, 512)
        weight_grad = last(
            left(*ORDER[-1]), *right(*ORDER[-1], name), total, h, weight_grad, 512
        )
    moment, params = outer.results()
    return weight_grad, moment, params


def solution(mesh):
    placed = (
        P("replica", "fsdp", None),
        P("replica", "fsdp", None),
        P("replica", "fsdp", None),
        P("fsdp", None),
        P("fsdp", "replica"),
    )
    return jax.shard_map(
        on_device,
        mesh=mesh,
        in_specs=placed,
        out_specs=(P("replica", "fsdp", None), P("fsdp", "replica"), P("fsdp", None)),
        check_vma=False,
    )
```

```python
import jax
import jax.numpy as jnp
from jax import lax
from jax.experimental import pallas as pl
from jax.experimental.pallas import tpu as pltpu
from jax.sharding import PartitionSpec as P

outer_mu = 0.9
outer_lr = 0.7

NY, NZ = 4, 4
COLUMNS = 4096
UNITS = 896
TOK = 128
LANES = 128
REPLICAS = 16
VMEM = 18 * 1024 * 1024


def shift(dy, dz):
    return [
        (y * NZ + z, (y + dy) % NY * NZ + (z + dz) % NZ)
        for y in range(NY)
        for z in range(NZ)
    ]


def fsdp_send(array, dy, dz):
    return lax.ppermute(array, "fsdp", shift(dy, dz))


def activate_kernel(place_ref, *refs):
    for source, target in zip(refs[:NY], refs[NY:]):
        value = source[0].astype(jnp.float32)
        value = value / (1.0 + jnp.exp(-value))
        target[0] = value.T.astype(jnp.bfloat16)


def activate(pre_act, place):
    def column(d):
        return lambda j, p: (0, 0, (p[0] + d) % NY * NZ + (p[1] + j) % NZ)

    return pl.pallas_call(
        activate_kernel,
        grid_spec=pltpu.PrefetchScalarGridSpec(
            num_scalar_prefetch=1,
            grid=(NZ,),
            in_specs=[pl.BlockSpec((1, TOK, UNITS), column(d)) for d in range(NY)],
            out_specs=[
                pl.BlockSpec((1, UNITS, TOK), lambda j, p: (j, 0, 0))
                for _ in range(NY)
            ],
        ),
        out_shape=[jax.ShapeDtypeStruct((NZ, UNITS, TOK), jnp.bfloat16)] * NY,
        compiler_params=pltpu.CompilerParams(vmem_limit_bytes=VMEM),
    )(place, *[pre_act] * NY)


def matmul_kernel(lefts, rights, total, out_ref, packed):
    @pl.when(pl.program_id(0) == 0)
    def _():
        for i, source in enumerate(lefts):
            packed[:, i * TOK : (i + 1) * TOK] = source[0]

    right = jnp.concatenate([r[0] for r in rights], axis=0)
    value = jnp.dot(packed[...], right, preferred_element_type=jnp.float32)
    if total is not None:
        value = value + total[0]
    out_ref[0] = value.astype(out_ref.dtype)


def matmul(blocks, token, total=None, final=False, width=512):
    lefts = [(array, row) for array, row, _ in blocks]
    rights = [r for _, _, parts in blocks for r in parts]
    n, m, depth = len(lefts), len(rights), len(lefts) * TOK
    tile = pl.BlockSpec((1, UNITS, width), lambda i: (0, 0, i))
    operands = [a for a, _ in lefts] + rights + [token]
    in_specs = [
        pl.BlockSpec((1, UNITS, TOK), lambda i, row=row: (row, 0, 0)) for _, row in lefts
    ]
    in_specs += [pl.BlockSpec((1, r.shape[1], width), lambda i: (0, 0, i)) for r in rights]
    in_specs += [pl.BlockSpec(memory_space=pl.ANY)]
    alias = {}
    if total is not None:
        operands.append(total)
        in_specs.append(tile)
        if not final:
            alias = {n + m + 1: 0}

    def kernel(*refs):
        out_ref, token_ref, packed = refs[-3:]
        extra = refs[n + m + 1] if total is not None else None
        matmul_kernel(refs[:n], refs[n : n + m], extra, out_ref, packed)
        token_ref[...] = jnp.zeros_like(token_ref)

    return pl.pallas_call(
        kernel,
        grid=(COLUMNS // width,),
        in_specs=in_specs,
        out_specs=[tile, pl.BlockSpec((8, LANES), lambda i: (0, 0))],
        out_shape=[
            jax.ShapeDtypeStruct(
                (1, UNITS, COLUMNS), jnp.bfloat16 if final else jnp.float32
            ),
            jax.ShapeDtypeStruct((8, LANES), jnp.float32),
        ],
        input_output_aliases=alias,
        scratch_shapes=[pltpu.VMEM((UNITS, depth), jnp.bfloat16)],
        compiler_params=pltpu.CompilerParams(vmem_limit_bytes=VMEM),
        cost_estimate=pl.CostEstimate(
            flops=2 * UNITS * COLUMNS * depth,
            bytes_accessed=UNITS * COLUMNS * 4 + depth * (COLUMNS + UNITS) * 2,
            transcendentals=0,
        ),
    )(*operands)


def reduce_shares(pseudo_grads):
    pieces = pseudo_grads.reshape(REPLICAS, 32, LANES)
    return lax.all_to_all(pieces, "replica", 0, 0, tiled=True)


def outer_update(pieces, outer_params, momentum):
    share = momentum.shape[1]
    index = lax.axis_index("replica")
    delta = jnp.sum(pieces, axis=0).reshape(-1) / REPLICAS
    moment = outer_mu * momentum[0] + delta
    old = lax.dynamic_slice_in_dim(outer_params[0], index * share, share, 0)
    return moment, old - outer_lr * (delta + outer_mu * moment)


def hand_out(updated):
    copies = jnp.broadcast_to(updated.reshape(1, 32, LANES), (REPLICAS, 32, LANES))
    return lax.all_to_all(copies, "replica", 0, 0, tiled=True)


def on_device(pre_act, out_grad, pseudo_grads, outer_params, momentum):
    fsdp = lax.axis_index("fsdp")
    place = jnp.stack([fsdp // NZ, fsdp % NZ]).astype(jnp.int32)
    env = {"b0": out_grad, "token": jnp.zeros((8, LANES), jnp.float32)}

    def past(*values):
        env["token"], *values = lax.optimization_barrier((env["token"], *values))
        return values

    def event(done, start):
        sources = [make() for _, make, _, _ in start]
        held = past(*sources, *[env[name] for name in done])
        env.update(zip(done, held[len(sources) :]))
        for (name, _, dy, dz), source in zip(start, held):
            env[name] = fsdp_send(source, dy, dz)

    def up(k):
        return (f"p{k}", lambda: env[f"b{k}"], 1, 0)

    def down(k):
        return (f"m{k}", lambda: env[f"b{k}"], -1, 0)

    def far(k, step):
        return (f"f{k}", lambda: env[("p" if step > 0 else "m") + str(k)], step, 0)

    def along(k):
        return (f"b{k}", lambda: env[f"b{k - 1}"], 0, 1)

    def spread(s):
        return (f"X{s}", lambda: jnp.stack([env[f"R{d}"][s] for d in every]), 0, s)

    def compute(name, pairs, total=None, final=False):
        blocks = []
        for k, d in pairs:
            array, row = (env[f"R{d}"], 0) if k == 0 else (env[f"X{k}"], d)
            names = [("b", "p", "f", "m")[d] + str(k)]
            right = [env[part] for part in names]
            blocks.append((array, row, right))
        env[name], env["token"] = matmul(blocks, env["token"], total, final)

    every = range(NY)
    event([], [along(1), down(0), up(0)])
    (held,) = past(pre_act)
    env["R0"], env["o1"], env["o2"], env["o3"] = activate(held, place)
    event(
        [],
        [("q2", lambda: env["o2"], 1, 0), ("R3", lambda: env["o3"], -1, 0)],
    )
    event(["b1"], [along(2)])
    env["shares"] = reduce_shares(*past(pseudo_grads))
    event(["p0", "m0"], [("R1", lambda: env["o1"], 1, 0), far(0, -1)])
    event(["b2"], [along(3)])
    event(["q2", "R3"], [("R2", lambda: env["q2"], 1, 0), down(1)])
    event(["R1", "f0", "shares"], [up(1), down(2)])
    moment, updated = outer_update(env["shares"], outer_params, momentum)
    event(["R2", "m1", "b3"], [up(2), far(1, -1), spread(1)])
    env["params"] = hand_out(*past(updated))
    event(["p1", "m2", "X1"], [up(3), down(3), spread(2)])
    event(["p2", "f1", "params"], [far(2, 1)])
    compute("t1", [(k, d) for k in (0, 1) for d in every])
    event(["X2"], [spread(3)])
    event(["m3"], [far(3, -1)])
    compute("t2", [(2, d) for d in (0, 1, 3)], env["t1"])
    event(["p3", "f2", "X3", "f3"], [])
    compute("out", [(2, 2), (3, 0), (3, 1), (3, 2), (3, 3)], env["t2"], final=True)
    return env["out"], moment[None], env["params"].reshape(1, -1)


def solution(mesh):
    placed = (
        P("replica", "fsdp", None),
        P("replica", "fsdp", None),
        P("replica", "fsdp", None),
        P("fsdp", None),
        P("fsdp", "replica"),
    )
    return jax.shard_map(
        on_device,
        mesh=mesh,
        in_specs=placed,
        out_specs=(P("replica", "fsdp", None), P("fsdp", "replica"), P("fsdp", None)),
        check_vma=False,
    )
```

```python
import jax
import jax.numpy as jnp
from jax import lax
from jax.experimental import pallas as pl
from jax.experimental.pallas import tpu as pltpu
from jax.sharding import PartitionSpec as P

outer_mu = 0.9
outer_lr = 0.7

NY, NZ = 4, 4
COLUMNS = 4096
UNITS = 896
TOK = 128
LANES = 128
REPLICAS = 16
VMEM = 18 * 1024 * 1024


def shift(dy, dz):
    return [
        (y * NZ + z, (y + dy) % NY * NZ + (z + dz) % NZ)
        for y in range(NY)
        for z in range(NZ)
    ]


def fsdp_send(array, dy, dz):
    return lax.ppermute(array, "fsdp", shift(dy, dz))


def activate_kernel(place_ref, *refs):
    for source, target in zip(refs[:NY], refs[NY:]):
        value = source[0].astype(jnp.float32)
        value = value / (1.0 + jnp.exp(-value))
        target[0] = value.T.astype(jnp.bfloat16)


def activate(pre_act, place):
    def column(d):
        return lambda j, p: (0, 0, (p[0] + d) % NY * NZ + (p[1] + j) % NZ)

    return pl.pallas_call(
        activate_kernel,
        grid_spec=pltpu.PrefetchScalarGridSpec(
            num_scalar_prefetch=1,
            grid=(NZ,),
            in_specs=[pl.BlockSpec((1, TOK, UNITS), column(d)) for d in range(NY)],
            out_specs=[
                pl.BlockSpec((1, UNITS, TOK), lambda j, p: (j, 0, 0))
                for _ in range(NY)
            ],
        ),
        out_shape=[jax.ShapeDtypeStruct((NZ, UNITS, TOK), jnp.bfloat16)] * NY,
        compiler_params=pltpu.CompilerParams(vmem_limit_bytes=VMEM),
    )(place, *[pre_act] * NY)


def matmul_kernel(lefts, rights, total, out_ref, packed):
    @pl.when(pl.program_id(0) == 0)
    def _():
        for i, source in enumerate(lefts):
            packed[:, i * TOK : (i + 1) * TOK] = source[0]

    right = jnp.concatenate([r[0] for r in rights], axis=0)
    value = jnp.dot(packed[...], right, preferred_element_type=jnp.float32)
    if total is not None:
        value = value + total[0]
    out_ref[0] = value.astype(out_ref.dtype)


def matmul(blocks, token, total=None, final=False, width=512):
    lefts = [(array, row) for array, row, _ in blocks]
    rights = [r for _, _, parts in blocks for r in parts]
    n, m, depth = len(lefts), len(rights), len(lefts) * TOK
    tile = pl.BlockSpec((1, UNITS, width), lambda i: (0, 0, i))
    operands = [a for a, _ in lefts] + rights + [token]
    in_specs = [
        pl.BlockSpec((1, UNITS, TOK), lambda i, row=row: (row, 0, 0)) for _, row in lefts
    ]
    in_specs += [pl.BlockSpec((1, r.shape[1], width), lambda i: (0, 0, i)) for r in rights]
    in_specs += [pl.BlockSpec(memory_space=pl.ANY)]
    alias = {}
    if total is not None:
        operands.append(total)
        in_specs.append(tile)
        if not final:
            alias = {n + m + 1: 0}

    def kernel(*refs):
        out_ref, token_ref, packed = refs[-3:]
        extra = refs[n + m + 1] if total is not None else None
        matmul_kernel(refs[:n], refs[n : n + m], extra, out_ref, packed)
        token_ref[...] = jnp.zeros_like(token_ref)

    return pl.pallas_call(
        kernel,
        grid=(COLUMNS // width,),
        in_specs=in_specs,
        out_specs=[tile, pl.BlockSpec((8, LANES), lambda i: (0, 0))],
        out_shape=[
            jax.ShapeDtypeStruct(
                (1, UNITS, COLUMNS), jnp.bfloat16 if final else jnp.float32
            ),
            jax.ShapeDtypeStruct((8, LANES), jnp.float32),
        ],
        input_output_aliases=alias,
        scratch_shapes=[pltpu.VMEM((UNITS, depth), jnp.bfloat16)],
        compiler_params=pltpu.CompilerParams(vmem_limit_bytes=VMEM),
        cost_estimate=pl.CostEstimate(
            flops=2 * UNITS * COLUMNS * depth,
            bytes_accessed=UNITS * COLUMNS * 4 + depth * (COLUMNS + UNITS) * 2,
            transcendentals=0,
        ),
    )(*operands)


def reduce_shares(pseudo_grads):
    pieces = pseudo_grads.reshape(REPLICAS, 32, LANES)
    return lax.all_to_all(pieces, "replica", 0, 0, tiled=True)


def outer_update(pieces, outer_params, momentum):
    share = momentum.shape[1]
    index = lax.axis_index("replica")
    delta = jnp.sum(pieces, axis=0).reshape(-1) / REPLICAS
    moment = outer_mu * momentum[0] + delta
    old = lax.dynamic_slice_in_dim(outer_params[0], index * share, share, 0)
    return moment, old - outer_lr * (delta + outer_mu * moment)


def hand_out(updated):
    copies = jnp.broadcast_to(updated.reshape(1, 32, LANES), (REPLICAS, 32, LANES))
    return lax.all_to_all(copies, "replica", 0, 0, tiled=True)


def on_device(pre_act, out_grad, pseudo_grads, outer_params, momentum):
    fsdp = lax.axis_index("fsdp")
    place = jnp.stack([fsdp // NZ, fsdp % NZ]).astype(jnp.int32)
    env = {"b0": out_grad, "token": jnp.zeros((8, LANES), jnp.float32)}

    def past(*values):
        env["token"], *values = lax.optimization_barrier((env["token"], *values))
        return values

    def event(done, start):
        sources = [make() for _, make, _, _ in start]
        held = past(*sources, *[env[name] for name in done])
        env.update(zip(done, held[len(sources) :]))
        for (name, _, dy, dz), source in zip(start, held):
            env[name] = fsdp_send(source, dy, dz)

    def up(k):
        return (f"p{k}", lambda: env[f"b{k}"], 1, 0)

    def down(k):
        return (f"m{k}", lambda: env[f"b{k}"], -1, 0)

    def far(k, step):
        return (f"f{k}", lambda: env[("p" if step > 0 else "m") + str(k)], step, 0)

    def along(k):
        return (f"b{k}", lambda: env[f"b{k - 1}"], 0, 1)

    def spread(s, near=range(NY), name=""):
        def packed():
            return jnp.stack([env[f"R{d}"][s] for d in near])

        for i, d in enumerate(near):
            where[s, d] = (f"X{s}{name}", i)
        return (f"X{s}{name}", packed, 0, s)

    where = {(0, d): (f"R{d}", 0) for d in range(NY)}

    def compute(name, pairs, total=None, final=False):
        blocks = []
        for k, d in pairs:
            array, row = where[k, d]
            part = ("b", "p", "f", "m")[d] + str(k)
            right = [env[part]] if part in env else [env[part + "y"], env[part + "z"]]
            blocks.append((env[array], row, right))
        env[name], env["token"] = matmul(blocks, env["token"], total, final)

    every = range(NY)
    event([], [along(1), down(0), up(0)])
    (held,) = past(pre_act)
    env["R0"], env["o1"], env["o2"], env["o3"] = activate(held, place)
    event(
        [],
        [("q2", lambda: env["o2"], 1, 0), ("R3", lambda: env["o3"], -1, 0)],
    )
    event(["b1"], [along(2)])
    env["shares"] = reduce_shares(*past(pseudo_grads))
    event(["p0", "m0"], [("R1", lambda: env["o1"], 1, 0), far(0, -1)])
    event(["b2"], [along(3)])
    event(["q2", "R3"], [("R2", lambda: env["q2"], 1, 0), down(1)])
    event(["R1", "f0", "shares"], [up(1), down(2)])
    moment, updated = outer_update(env["shares"], outer_params, momentum)
    event(["R2"], [spread(1), up(2)])
    event(["m1", "b3"], [far(1, -1)])
    env["params"] = hand_out(*past(updated))
    event(["p1", "m2", "X1"], [up(3), down(3), spread(2)])
    event(["p2", "f1", "params"], [far(2, 1)])
    env["params"] = env["params"].reshape(1, -1)
    compute("t1", [(k, d) for k in (0, 1) for d in every])
    event(["m3"], [far(3, -1)])
    event(["X2"], [spread(3)])
    compute("t2", [(2, d) for d in (0, 1, 3)], env["t1"])
    event(["f2", "p3"], [])
    compute("t3", [(2, 2)], env["t2"])
    event(["X3", "f3", "params"], [])
    compute("out", [(3, 0), (3, 1), (3, 2), (3, 3)], env["t3"], final=True)
    return env["out"], moment[None], env["params"]


def solution(mesh):
    placed = (
        P("replica", "fsdp", None),
        P("replica", "fsdp", None),
        P("replica", "fsdp", None),
        P("fsdp", None),
        P("fsdp", "replica"),
    )
    return jax.shard_map(
        on_device,
        mesh=mesh,
        in_specs=placed,
        out_specs=(P("replica", "fsdp", None), P("fsdp", "replica"), P("fsdp", None)),
        check_vma=False,
    )
```

```python
import jax
import jax.numpy as jnp
from jax import lax
from jax.experimental import pallas as pl
from jax.experimental.pallas import tpu as pltpu
from jax.sharding import PartitionSpec as P

outer_mu = 0.9
outer_lr = 0.7

NY, NZ = 4, 4
COLUMNS = 4096
UNITS = 896
TOK = 128
LANES = 128
REPLICAS = 16
VMEM = 18 * 1024 * 1024


def shift(dy, dz):
    return [
        (y * NZ + z, (y + dy) % NY * NZ + (z + dz) % NZ)
        for y in range(NY)
        for z in range(NZ)
    ]


def fsdp_send(array, dy, dz):
    return lax.ppermute(array, "fsdp", shift(dy, dz))


def activate_kernel(place_ref, *refs):
    for source, target in zip(refs[:NY], refs[NY:]):
        value = source[0].astype(jnp.float32)
        value = value / (1.0 + jnp.exp(-value))
        target[0] = value.T.astype(jnp.bfloat16)


def activate(pre_act, place):
    def column(d):
        return lambda j, p: (0, 0, (p[0] + d) % NY * NZ + (p[1] + j) % NZ)

    return pl.pallas_call(
        activate_kernel,
        grid_spec=pltpu.PrefetchScalarGridSpec(
            num_scalar_prefetch=1,
            grid=(NZ,),
            in_specs=[pl.BlockSpec((1, TOK, UNITS), column(d)) for d in range(NY)],
            out_specs=[
                pl.BlockSpec((1, UNITS, TOK), lambda j, p: (j, 0, 0))
                for _ in range(NY)
            ],
        ),
        out_shape=[jax.ShapeDtypeStruct((NZ, UNITS, TOK), jnp.bfloat16)] * NY,
        compiler_params=pltpu.CompilerParams(vmem_limit_bytes=VMEM),
    )(place, *[pre_act] * NY)


def matmul_kernel(lefts, rights, total, out_ref, packed):
    @pl.when(pl.program_id(0) == 0)
    def _():
        for i, source in enumerate(lefts):
            packed[:, i * TOK : (i + 1) * TOK] = source[0]

    right = jnp.concatenate([r[0] for r in rights], axis=0)
    value = jnp.dot(packed[...], right, preferred_element_type=jnp.float32)
    if total is not None:
        value = value + total[0]
    out_ref[0] = value.astype(out_ref.dtype)


def matmul(blocks, token, total=None, final=False, width=512):
    lefts = [(array, row) for array, row, _ in blocks]
    rights = [r for _, _, parts in blocks for r in parts]
    n, m, depth = len(lefts), len(rights), len(lefts) * TOK
    tile = pl.BlockSpec((1, UNITS, width), lambda i: (0, 0, i))
    operands = [a for a, _ in lefts] + rights + [token]
    in_specs = [
        pl.BlockSpec((1, UNITS, TOK), lambda i, row=row: (row, 0, 0)) for _, row in lefts
    ]
    in_specs += [pl.BlockSpec((1, r.shape[1], width), lambda i: (0, 0, i)) for r in rights]
    in_specs += [pl.BlockSpec(memory_space=pl.ANY)]
    alias = {}
    if total is not None:
        operands.append(total)
        in_specs.append(pl.BlockSpec(memory_space=pltpu.VMEM) if final else tile)
        if not final:
            alias = {n + m + 1: 0}

    def kernel(*refs):
        out_ref, token_ref, packed = refs[-3:]
        extra = refs[n + m + 1] if total is not None else None
        if final:
            first = pl.multiple_of(pl.program_id(0) * width, width)
            extra = extra.at[:, :, pl.ds(first, width)]
        matmul_kernel(refs[:n], refs[n : n + m], extra, out_ref, packed)
        token_ref[...] = jnp.zeros_like(token_ref)

    return pl.pallas_call(
        kernel,
        grid=(COLUMNS // width,),
        in_specs=in_specs,
        out_specs=[tile, pl.BlockSpec((8, LANES), lambda i: (0, 0))],
        out_shape=[
            jax.ShapeDtypeStruct(
                (1, UNITS, COLUMNS), jnp.bfloat16 if final else jnp.float32
            ),
            jax.ShapeDtypeStruct((8, LANES), jnp.float32),
        ],
        input_output_aliases=alias,
        scratch_shapes=[pltpu.VMEM((UNITS, depth), jnp.bfloat16)],
        compiler_params=pltpu.CompilerParams(vmem_limit_bytes=VMEM),
        cost_estimate=pl.CostEstimate(
            flops=2 * UNITS * COLUMNS * depth,
            bytes_accessed=UNITS * COLUMNS * 4 + depth * (COLUMNS + UNITS) * 2,
            transcendentals=0,
        ),
    )(*operands)


def reduce_shares(pseudo_grads):
    pieces = pseudo_grads.reshape(REPLICAS, 32, LANES)
    return lax.all_to_all(pieces, "replica", 0, 0, tiled=True)


def outer_update(pieces, outer_params, momentum):
    share = momentum.shape[1]
    index = lax.axis_index("replica")
    delta = jnp.sum(pieces, axis=0).reshape(-1) / REPLICAS
    moment = outer_mu * momentum[0] + delta
    old = lax.dynamic_slice_in_dim(outer_params[0], index * share, share, 0)
    return moment, old - outer_lr * (delta + outer_mu * moment)


def hand_out(updated):
    copies = jnp.broadcast_to(updated.reshape(1, 32, LANES), (REPLICAS, 32, LANES))
    return lax.all_to_all(copies, "replica", 0, 0, tiled=True)


def on_device(pre_act, out_grad, pseudo_grads, outer_params, momentum):
    fsdp = lax.axis_index("fsdp")
    place = jnp.stack([fsdp // NZ, fsdp % NZ]).astype(jnp.int32)
    env = {"b0": out_grad, "token": jnp.zeros((8, LANES), jnp.float32)}

    def past(*values):
        env["token"], *values = lax.optimization_barrier((env["token"], *values))
        return values

    def event(done, start):
        sources = [make() for _, make, _, _ in start]
        held = past(*sources, *[env[name] for name in done])
        env.update(zip(done, held[len(sources) :]))
        for (name, _, dy, dz), source in zip(start, held):
            env[name] = fsdp_send(source, dy, dz)

    def up(k):
        return (f"p{k}", lambda: env[f"b{k}"], 1, 0)

    def down(k):
        return (f"m{k}", lambda: env[f"b{k}"], -1, 0)

    def far(k, step):
        return (f"f{k}", lambda: env[("p" if step > 0 else "m") + str(k)], step, 0)

    def along(k):
        return (f"b{k}", lambda: env[f"b{k - 1}"], 0, 1)

    def spread(s, near=range(NY), name=""):
        def packed():
            return jnp.stack([env[f"R{d}"][s] for d in near])

        for i, d in enumerate(near):
            where[s, d] = (f"X{s}{name}", i)
        return (f"X{s}{name}", packed, 0, s)

    where = {(0, d): (f"R{d}", 0) for d in range(NY)}

    def compute(name, pairs, total=None, final=False):
        blocks = []
        for k, d in pairs:
            array, row = where[k, d]
            part = ("b", "p", "f", "m")[d] + str(k)
            right = [env[part]] if part in env else [env[part + "y"], env[part + "z"]]
            blocks.append((env[array], row, right))
        env[name], env["token"] = matmul(blocks, env["token"], total, final, 1024 if final else 512)

    every = range(NY)
    event([], [along(1), down(0), up(0)])
    (held,) = past(pre_act)
    env["R0"], env["o1"], env["o2"], env["o3"] = activate(held, place)
    event(
        [],
        [("q2", lambda: env["o2"], 1, 0), ("R3", lambda: env["o3"], -1, 0)],
    )
    event(["b1"], [along(2)])
    env["shares"] = reduce_shares(*past(pseudo_grads))
    event(["p0", "m0"], [("R1", lambda: env["o1"], 1, 0), far(0, -1)])
    event(["b2"], [along(3)])
    event(["q2", "R3"], [("R2", lambda: env["q2"], 1, 0), down(1)])
    event(["R1", "f0", "shares"], [up(1), down(2)])
    moment, updated = outer_update(env["shares"], outer_params, momentum)
    event(["R2"], [spread(1), up(2)])
    event(["m1", "b3"], [far(1, -1)])
    env["params"] = hand_out(*past(updated))
    event(["p1", "m2", "X1"], [up(3), down(3), spread(2)])
    event(["p2", "f1", "params"], [far(2, 1)])
    env["params"] = env["params"].reshape(1, -1)
    compute("t1", [(k, d) for k in (0, 1) for d in every])
    event(["m3"], [far(3, -1)])
    event(["X2"], [spread(3)])
    compute("t2", [(2, d) for d in (0, 1, 3)], env["t1"])
    event(["f2", "p3"], [])
    compute("t3", [(2, 2)], env["t2"])
    event(["X3", "f3", "params"], [])
    compute("out", [(3, 0), (3, 1), (3, 2), (3, 3)], env["t3"], final=True)
    return env["out"], moment[None], env["params"]


def solution(mesh):
    placed = (
        P("replica", "fsdp", None),
        P("replica", "fsdp", None),
        P("replica", "fsdp", None),
        P("fsdp", None),
        P("fsdp", "replica"),
    )
    return jax.shard_map(
        on_device,
        mesh=mesh,
        in_specs=placed,
        out_specs=(P("replica", "fsdp", None), P("fsdp", "replica"), P("fsdp", None)),
        check_vma=False,
    )
```
